32 devices in a mesh: blk: 8 (over z, x), rep: 4 (over y, core).
Axes of the slice: x: 2, y: 2, z: 4, core: 2. Of those that a mesh axis runs over, the one named last changes fastest.
Arguments:
- images: bfloat16 [1024, 4, 4, 256], P(('blk', 'rep')), may hold values from -8 to 8
- conv_weight: bfloat16 [3, 3, 8, 256], replicated, may hold values from -0.75 to 0.75
- projection: bfloat16 [256, 512], replicated, may hold values from -0.375 to 0.375
- row_of: int32 [1024], P('blk'), may hold values from 0 to 1023, as said below
- probes: float32 [1024, 32], P(('blk', 'rep')), may hold values from -6 to 6
- initial: float32 [1024, 32], P(('blk', 'rep')), may hold values from -4 to 4
- amplitude: float32 [1], replicated, may hold values from 0.5 to 2
- inv_scale: float32 [1], replicated, may hold values from 3 to 8
- noise_var: float32 [1], replicated, may hold values from 0.5 to 2
Outputs:
- solution: float32 [1024, 32], P(('blk', 'rep'))
- residual: float32 [1024, 32], P(('blk', 'rep'))
The draws below stay inside these ranges and needn't reach their ends.
Inputs may be any that keep to these rules, and one draw needn't show every extreme that they name: row_of is a permutation of the 1024 rows. Row block k holds rows k * 128 to (k + 1) * 128 - 1. The 128 patches of the devices that share a blk index go to 8 distinct row blocks, 16 to each, and every row block receives exactly 128 patches.
All inputs are finite; a program needn't handle non-finite values.
Results may differ from the reference program's by a relative error of at most 0.0024.
Values may be sent and summed in bfloat16 or wider, within the bound.
A program may use at most 64 MiB of HBM per device.

```python
import math
import jax
import jax.numpy as jnp
from jax import lax

F = 512
CH = 256
GROUPS = 32
SIDE = 4
PROBES = 32
ITERS = 2
ROWS = 128
N = 1024
DESTS = 8
PER = 16
N_BLK = 8


def draw_images(key, part):
    key = jax.random.fold_in(key, 5)
    label_key, centre_key, weight_key, noise_key = jax.random.split(key, 4)
    cluster_count = max(N // 16, 1)
    labels = jax.random.randint(label_key, (N,), 0, cluster_count)
    centres = jax.random.normal(centre_key, (cluster_count, CH), jnp.float32)
    strength = jnp.exp(jax.random.uniform(weight_key, (N,), jnp.float32, math.log(0.15), math.log(1.2)))
    noise = jax.random.normal(noise_key, (N, SIDE, SIDE, CH), jnp.float32)
    picked = centres[labels]
    images = strength[:, None, None, None] * picked[:, None, None, :] + noise
    return jnp.clip(images, -8.0, 8.0).astype(jnp.bfloat16)


def draw_row_of(key, part):
    key = jax.random.fold_in(key, 11)
    first_key, second_key, third_key = jax.random.split(key, 3)
    offsets = jax.random.permutation(first_key, N_BLK)[:DESTS]
    arrival = jax.vmap(lambda subkey: jax.random.permutation(subkey, ROWS))(jax.random.split(second_key, N_BLK))
    within = jax.vmap(lambda subkey: jax.random.permutation(subkey, ROWS))(jax.random.split(third_key, N_BLK))
    source_blk = jnp.arange(N_BLK, dtype=jnp.int32)[:, None]
    target_blk = (source_blk + offsets[arrival // PER]) % N_BLK
    local_row = within[target_blk, arrival]
    rows = target_blk * ROWS + local_row
    return rows.reshape(-1).astype(jnp.int32)


def levels(key, extent, shards, smallest, top_value):
    def one(axis_at, blocks):
        draws = jax.random.uniform(jax.random.fold_in(jax.random.fold_in(key, 6), axis_at), (blocks,), jnp.float32, smallest / len(shards), top_value / len(shards))
        return jnp.repeat(jnp.exp(draws), extent[axis_at] // blocks).reshape((-1,) + (1,) * (len(extent) - axis_at - 1))

    level = one(*shards[0])
    for cut in shards[1:]:
        level = level * one(*cut)
    return level


def bell_draw(rng, shape, spread, reach, pieces=(), held_as=jnp.bfloat16):
    level = levels(rng, shape, pieces, -0.22, 0.18) if pieces else 1.0
    entries = jax.random.normal(rng, shape, jnp.float32) * spread * level
    return jnp.minimum(jnp.maximum(entries, -reach), reach).astype(held_as)


def setup_inputs(seed: int = 0) -> dict:
    keys = jax.random.split(jax.random.key(seed), 10)
    images = draw_images(jax.random.fold_in(keys[9], 71), 0)
    conv_weight = bell_draw(keys[1], (3, 3, CH // GROUPS, CH), (9 * (CH // GROUPS)) ** -0.5, 0.75)
    projection = bell_draw(keys[2], (CH, F), CH ** -0.5, 0.375)
    row_of = draw_row_of(jax.random.fold_in(keys[9], 71), 0)
    probes = bell_draw(keys[4], (N, PROBES), 1.0, 6.0, ((0, 32),), jnp.float32)
    initial = bell_draw(keys[5], (N, PROBES), 0.3, 4.0, ((0, 32),), jnp.float32)
    amplitude = jnp.clip(jnp.exp(jax.random.uniform(keys[6], (1,), jnp.float32, math.log(0.5), math.log(2.0))), 0.5, 2.0)
    inv_scale = jnp.clip(jnp.exp(jax.random.uniform(keys[7], (1,), jnp.float32, math.log(3.0), math.log(8.0))), 3.0, 8.0)
    noise_var = jnp.clip(jnp.exp(jax.random.uniform(keys[8], (1,), jnp.float32, math.log(0.5), math.log(2.0))), 0.5, 2.0)
    return {"images": images, "conv_weight": conv_weight, "projection": projection, "row_of": row_of, "probes": probes, "initial": initial, "amplitude": amplitude, "inv_scale": inv_scale, "noise_var": noise_var}


def encode(images, conv_weight, projection):
    conv_out = lax.conv_general_dilated(images, conv_weight, (1, 1), 'SAME', dimension_numbers=('NHWC', 'HWIO', 'NHWC'), feature_group_count=GROUPS, preferred_element_type=jnp.float32)
    mixed = images.astype(jnp.float32) + jax.nn.silu(conv_out)
    pooled = lax.optimization_barrier(jnp.mean(mixed, axis=(1, 2))).astype(jnp.bfloat16)
    raw_proj = jnp.dot(pooled, projection, preferred_element_type=jnp.float32)
    inverse = lax.rsqrt(lax.optimization_barrier(jnp.mean(raw_proj * raw_proj, axis=-1, keepdims=True)) + 1e-05)
    return (raw_proj * inverse).astype(jnp.bfloat16)

def kernel_rows(row_feats, row_norms, col_feats, col_norms, amplitude, inv_scale):
    cross = lax.dot_general(col_feats, row_feats, (((1,), (1,)), ((), ())), preferred_element_type=jnp.float32)
    distance = col_norms[:, None] + row_norms[None, :] - 2.0 * cross
    return amplitude * jnp.exp(-inv_scale * distance / (2.0 * F))

def contract(kern, vectors):
    return lax.dot_general(kern, vectors, (((0,), (0,)), ((), ())), precision=lax.Precision.HIGHEST, preferred_element_type=jnp.float32)

def column_dots(left, right):
    return lax.optimization_barrier(jnp.sum(left * right, axis=0))

def reference(images, conv_weight, projection, row_of, probes, initial, amplitude, inv_scale, noise_var):
    encoded = encode(images, conv_weight, projection)
    placed = jnp.zeros((N, F), jnp.bfloat16).at[row_of].set(encoded)
    wide = placed.astype(jnp.float32)
    norms = lax.optimization_barrier(jnp.sum(wide * wide, axis=1))
    block_rows = math.gcd(N, 512)
    blocks = placed.reshape(N // block_rows, block_rows, F)
    norm_blocks = norms.reshape(N // block_rows, block_rows)

    def product(vectors):

        def one_block(pair):
            kern = kernel_rows(pair[0], pair[1], placed, norms, amplitude, inv_scale)
            return contract(kern, vectors)
        result = lax.map(one_block, (blocks, norm_blocks)).reshape(N, PROBES)
        return result + noise_var * vectors
    solution = initial
    residual = probes - product(initial)
    direction = residual
    norm_now = column_dots(residual, residual)
    for iteration in range(ITERS):
        image = product(direction)
        alpha = norm_now / column_dots(direction, image)
        solution = solution + alpha * direction
        residual = residual - alpha * image
        norm_next = column_dots(residual, residual)
        direction = residual + norm_next / norm_now * direction
        norm_now = norm_next
    return (solution, residual)
```

```python
import jax
import jax.numpy as jnp
from jax import lax
from jax.sharding import PartitionSpec as P
from jax.experimental import pallas as pl
from jax.experimental.pallas import tpu as pltpu

F = 512
GROUPS = 32
ITERS = 2


def encode(images, conv_weight, projection):
    conv_out = lax.conv_general_dilated(
        images,
        conv_weight,
        (1, 1),
        "SAME",
        dimension_numbers=("NHWC", "HWIO", "NHWC"),
        feature_group_count=GROUPS,
        preferred_element_type=jnp.float32,
    )
    mixed = images.astype(jnp.float32) + jax.nn.silu(conv_out)
    pooled = jnp.mean(mixed, axis=(1, 2)).astype(jnp.bfloat16)
    raw_proj = jnp.dot(pooled, projection, preferred_element_type=jnp.float32)
    inverse = lax.rsqrt(jnp.mean(raw_proj * raw_proj, axis=-1, keepdims=True) + 1e-05)
    return (raw_proj * inverse).astype(jnp.bfloat16)


def kernel_rows(row_feats, row_norms, col_feats, col_norms, amplitude, inv_scale):
    cross = lax.dot_general(
        col_feats, row_feats, (((1,), (1,)), ((), ())), preferred_element_type=jnp.float32
    )
    distance = col_norms[:, None] + row_norms[None, :] - 2.0 * cross
    return amplitude * jnp.exp(-inv_scale * distance / (2.0 * F))


def contract(kern, vectors):
    return lax.dot_general(
        kern,
        vectors,
        (((0,), (0,)), ((), ())),
        precision=lax.Precision.HIGHEST,
        preferred_element_type=jnp.float32,
    )


def column_dots(left, right):
    return jnp.sum(left * right, axis=0)


def per_device(
    images, conv_weight, projection, row_of, probes, initial, amplitude, inv_scale, noise_var
):
    encoded = encode(images, conv_weight, projection)
    quarter = encoded.shape[0]
    group = lax.all_gather(encoded, "rep", axis=0, tiled=True)
    rows_total = group.shape[0]
    blk_count = lax.axis_size("blk")
    per_dest = rows_total // min(rows_total, blk_count)
    block_first = lax.axis_index("blk") * rows_total
    target_blk = row_of // rows_total
    order = jnp.arange(rows_total, dtype=jnp.int32)
    same_target = target_blk[:, None] == target_blk[None, :]
    earlier = order[None, :] < order[:, None]
    arrival = jnp.sum(jnp.logical_and(same_target, earlier).astype(jnp.int32), axis=1)
    chosen = jnp.logical_and(
        target_blk[None, None, :] == jnp.arange(blk_count, dtype=jnp.int32)[:, None, None],
        arrival[None, None, :] == jnp.arange(per_dest, dtype=jnp.int32)[None, :, None],
    )
    outgoing = jnp.einsum(
        "bsq,qf->bsf", chosen.astype(jnp.bfloat16), group, preferred_element_type=jnp.float32
    ).astype(jnp.bfloat16)
    row_slots = jnp.sum(jnp.where(chosen, row_of[None, None, :] + 1, 0), axis=2) - 1
    incoming, incoming_rows = (
        lax.all_to_all(outgoing, "blk", split_axis=0, concat_axis=0, tiled=True),
        lax.all_to_all(row_slots, "blk", split_axis=0, concat_axis=0, tiled=True),
    )
    local_pos = incoming_rows.reshape(-1) - block_first
    placing = (local_pos[None, :] == order[:, None]).astype(jnp.bfloat16)
    row_feats = jnp.dot(
        placing, incoming.reshape(-1, incoming.shape[-1]), preferred_element_type=jnp.float32
    ).astype(jnp.bfloat16)
    mine = lax.dynamic_slice_in_dim(row_feats, lax.axis_index("rep") * quarter, quarter, 0)
    row_wide = row_feats.astype(jnp.float32)
    row_norms = jnp.sum(row_wide * row_wide, axis=1)
    probe_count = probes.shape[1]
    zeros_acc = jnp.zeros((rows_total, probe_count), jnp.float32)

    def tile_of(segment):
        seg_wide = segment.astype(jnp.float32)
        return kernel_rows(
            row_feats,
            row_norms,
            segment,
            jnp.sum(seg_wide * seg_wide, axis=1),
            amplitude,
            inv_scale,
        )

    def finish(totals, vectors):
        return (
            lax.psum_scatter(totals, "rep", scatter_dimension=0, tiled=True) + noise_var * vectors
        )

    def columns(vectors):
        return lax.all_gather(vectors, "blk", axis=0, tiled=True)

    def product(vectors):
        gathered = columns(vectors)
        segment = lax.all_gather(mine, "blk", axis=0, tiled=True)
        vec_rows = lax.slice_in_dim(gathered, 0, segment.shape[0], axis=0)
        return finish(zeros_acc + contract(tile_of(segment), vec_rows), vectors)

    start_image = product(initial)

    def paired(vectors, image):
        return lax.psum(
            (column_dots(vectors, vectors), column_dots(vectors, image)), ("blk", "rep")
        )

    solution = initial
    residual = probes - start_image
    image = product(residual)
    norm_now, inner = paired(residual, image)
    alpha = norm_now / inner
    direction = residual
    along = image
    for iteration in range(ITERS):
        solution = solution + alpha * direction
        residual = residual - alpha * along
        if iteration + 1 < ITERS:
            image = product(residual)
            norm_next, inner = paired(residual, image)
            ratio = norm_next / norm_now
            alpha = norm_next / (inner - ratio * norm_next / alpha)
            direction = residual + ratio * direction
            along = image + ratio * along
            norm_now = norm_next
    return (solution, residual)


f32 = jnp.float32
bf16 = jnp.bfloat16
MESH = pl.DeviceIdType.MESH
LOG2E = 1.4426950408889634


class Gather:
    def __init__(self, buf, send, recv, where):
        self.buf, self.send, self.recv = buf, send, recv
        self.z, self.x, self.y, self.c = where
        self.q = (self.x * 2 + self.y) * 2 + self.c
        self.qx = ((1 - self.x) * 2 + self.y) * 2 + self.c
        self.qy = (self.x * 2 + (1 - self.y)) * 2 + self.c
        self.qd = ((1 - self.x) * 2 + (1 - self.y)) * 2 + self.c
        self.px = (self.z * 2 + 1 - self.x, self.y * 2 + self.c)
        self.py = (self.z * 2 + self.x, (1 - self.y) * 2 + self.c)
        self.pc = (self.z * 2 + self.x, self.y * 2 + 1 - self.c)
        self.copies = []

    def copy(self, k, ref, device):
        c = pltpu.make_async_remote_copy(
            src_ref=ref, dst_ref=ref, send_sem=self.send.at[k], recv_sem=self.recv.at[k],
            device_id=device, device_id_type=MESH)
        c.start()
        self.copies.append(c)
        return c

    def start_z(self):
        own = self.buf.at[self.q, self.z]
        self.zc = [
            self.copy(d - 1, own, (lax.rem(self.z + d, 4) * 2 + self.x, self.y * 2 + self.c))
            for d in (1, 2, 3)
        ]

    def start_xy(self):
        for c in self.zc:
            c.wait_recv()
        col = self.buf.at[self.q]
        self.cx = self.copy(3, col, self.px)
        self.cy = self.copy(4, col, self.py)
        self.cc = self.copy(5, col, self.pc)

    def forward(self):
        half = self.buf.shape[1] // 2
        self.cx.wait_recv()
        self.fy = self.copy(6, self.buf.at[self.qx, pl.ds(0, half)], self.py)
        self.ccx = self.copy(8, self.buf.at[self.qx], self.pc)
        self.cy.wait_recv()
        self.fx = self.copy(7, self.buf.at[self.qy, pl.ds(half, half)], self.px)
        self.ccy = self.copy(9, self.buf.at[self.qy], self.pc)

    def forward_diagonal(self):
        self.fy.wait_recv()
        self.fx.wait_recv()
        self.ccd = self.copy(10, self.buf.at[self.qd], self.pc)

    def finish(self):
        for c in (self.cc, self.ccx, self.ccy, self.ccd):
            c.wait_recv()

    def drain(self):
        for c in self.copies:
            c.wait_send()


def split(value):
    high = value.astype(bf16)
    return high, (value - high.astype(f32)).astype(bf16)


def whole_kernel(
    images, weight, projection, row_of, probes, initial, amp, inv, noise, sol_out, res_out,
    vbuf, pbuf, padded, wide_w, perm_v, feats, dcol, ehi, elo, whl, sol, res, direc, image,
    vsend, vrecv, psend, precv,
):
    blk, rep = lax.axis_index("blk"), lax.axis_index("rep")
    z, x = blk // 2, lax.rem(blk, 2)
    y, c = rep // 2, lax.rem(rep, 2)
    where = (z, x, y, c)
    vg = Gather(vbuf, vsend, vrecv, where)
    pg = Gather(pbuf, psend, precv, where)
    q = vg.q
    per = images.shape[0]
    rows = vbuf.shape[0] * vbuf.shape[1] * per
    tile = 256
    tiles = rows // tile
    first = blk * row_of.shape[1] + rep * per

    barrier = pltpu.get_barrier_semaphore()
    for d in (1, 2, 3):
        pl.semaphore_signal(
            barrier, inc=1, device_id=(lax.rem(z + d, 4) * 2 + x, rep), device_id_type=MESH)
    for device in (vg.px, vg.py, vg.pc):
        pl.semaphore_signal(barrier, inc=1, device_id=device, device_id_type=MESH)

    lane = lax.broadcasted_iota(jnp.int32, (per, row_of.shape[1]), 1)
    sub = lax.broadcasted_iota(jnp.int32, (per, row_of.shape[1]), 0)
    mine = jnp.sum(
        jnp.where(lane == sub + rep * per, row_of[...].astype(f32), 0.0), axis=1, keepdims=True)
    vbuf[q, z] = jnp.broadcast_to(mine, (per, 128))
    vbuf[q, z, :, 0:32] = probes[...]
    vbuf[q, z, :, 32:64] = initial[...]
    pl.semaphore_wait(barrier, 6)
    vg.start_z()

    channels = images.shape[3]
    group = weight.shape[2]
    diag = (lax.broadcasted_iota(jnp.int32, (channels, channels), 0) // group
            == lax.broadcasted_iota(jnp.int32, (channels, channels), 1) // group)
    for t in range(9):
        w = weight[t // 3, t % 3].astype(f32)
        w = jnp.broadcast_to(w[None], (channels // group, group, channels))
        w = w.reshape(channels, channels)
        wide_w[t * channels:(t + 1) * channels] = jnp.where(diag, w, 0.0).astype(bf16)
    pixels = per * 16
    padded[0:8] = jnp.zeros((8, channels), f32)
    padded[pixels + 8:pixels + 16] = jnp.zeros((8, channels), f32)
    padded[8:pixels + 8] = images[...].astype(f32).reshape(pixels, channels)
    pos = lax.broadcasted_iota(jnp.int32, (tile, channels), 0)
    pos_x, pos_y = lax.rem(pos, 4), lax.rem(pos, 16) // 4

    def conv_tile(t):
        parts = []
        for dy in (-1, 0, 1):
            for dx in (-1, 0, 1):
                part = padded[8 + t * tile + dy * 4 + dx:8 + (t + 1) * tile + dy * 4 + dx]
                ok = None
                if dx:
                    ok = pos_x != (0 if dx < 0 else 3)
                if dy:
                    oky = pos_y != (0 if dy < 0 else 3)
                    ok = oky if ok is None else jnp.logical_and(ok, oky)
                if ok is not None:
                    part = jnp.where(ok, part, 0.0)
                parts.append(part.astype(bf16))
        v = jnp.dot(jnp.concatenate(parts, axis=1), wide_w[...], preferred_element_type=f32)
        mixed = padded[8 + t * tile:8 + (t + 1) * tile] + v / (1.0 + jnp.exp(-v))
        pooled = jnp.sum(mixed.reshape(tile // 16, 16, channels), axis=1) * (1.0 / 16.0)
        pbuf[q, z, t * 16:(t + 1) * 16] = pooled.astype(bf16)

    conv_tile(0)
    vg.start_xy()
    conv_tile(1)
    pg.start_z()
    vg.forward()
    pg.start_xy()
    vg.forward_diagonal()
    vg.finish()
    pg.forward()

    vall = vbuf[...].reshape(rows, 128)
    high = vall.astype(bf16)
    low = vall - high.astype(f32)
    lanes = lax.broadcasted_iota(jnp.int32, (rows, 128), 1)
    perm_v[...] = jnp.where(lanes < 64, high.astype(f32), pltpu.roll(low, 64, 1)).astype(bf16)
    j = lax.broadcasted_iota(jnp.int32, (1, rows), 1)
    jq, jz = j // (4 * per), lax.rem(j // per, 4)
    row_id = ((jz * 2 + jq // 4) * row_of.shape[1] + lax.rem(jq, 4) * per + lax.rem(j, per))
    row_id = row_id.astype(f32)
    per_tile = tile // (4 * per)
    for i in range(tiles):
        here = vbuf[i * per_tile:(i + 1) * per_tile].reshape(tile, 128)
        hot = (here[:, 64:65] == row_id).astype(f32).astype(bf16)
        got = jnp.dot(hot, perm_v[...], preferred_element_type=f32)
        got = got + pltpu.roll(got, 64, 1)
        res[i * tile:(i + 1) * tile] = got[:, 0:32]
        sol[i * tile:(i + 1) * tile] = got[:, 32:64]

    pg.forward_diagonal()
    pg.finish()

    scale = inv[0] / (2.0 * feats.shape[1])
    for i in range(tiles):
        pooled = pbuf[i * per_tile:(i + 1) * per_tile].reshape(tile, channels)
        raw = jnp.dot(pooled, projection[...], preferred_element_type=f32)
        mean = jnp.sum(raw * raw, axis=1, keepdims=True) * (1.0 / raw.shape[1])
        enc = (raw * lax.rsqrt(mean + 1e-05)).astype(bf16)
        feats[i * tile:(i + 1) * tile] = enc
        enc = enc.astype(f32)
        sq = jnp.sum(enc * enc, axis=1, keepdims=True)
        dcol[i * tile:(i + 1) * tile] = jnp.broadcast_to(jnp.exp(-scale * sq), (tile, 32))

    gain = scale * (2.0 * LOG2E)

    @pl.loop(0, tiles)
    def _(i):
        r = pl.ds(pl.multiple_of(i * tile, tile), tile)
        for k in range(tiles):
            g = lax.dot_general(
                feats[r, :], feats[k * tile:(k + 1) * tile], (((1,), (1,)), ((), ())),
                preferred_element_type=f32)
            e = jnp.exp2(gain * g)
            high, low = split(e)
            ehi[r, k * tile:(k + 1) * tile] = high
            elo[r, k * tile:(k + 1) * tile] = low

    amplitude, noise_var = amp[0], noise[0]

    def product(vec):
        w = dcol[...] * vec[...]
        high, low = split(w)
        whl[:, 0:32] = high
        whl[:, 32:64] = low

        @pl.loop(0, tiles)
        def _(i):
            r = pl.ds(pl.multiple_of(i * tile, tile), tile)
            a = jnp.dot(ehi[r, :], whl[...], preferred_element_type=f32)
            b = jnp.dot(elo[r, :], whl[:, 0:32], preferred_element_type=f32)
            s = a[:, 0:32] + a[:, 32:64] + b
            image[r, :] = amplitude * (dcol[r, :] * s) + noise_var * vec[r, :]

    product(sol)
    first_res = res[...] - image[...]
    res[...] = first_res
    direc[...] = first_res
    norm = jnp.sum(first_res * first_res, axis=0, keepdims=True)
    for iteration in range(ITERS):
        product(direc)
        d = direc[...]
        im = image[...]
        alpha = norm / jnp.sum(d * im, axis=0, keepdims=True)
        sol[...] = sol[...] + alpha * d
        r = res[...] - alpha * im
        res[...] = r
        if iteration + 1 < ITERS:
            new = jnp.sum(r * r, axis=0, keepdims=True)
            direc[...] = r + (new / norm) * d
            norm = new

    shigh, slow = split(sol[...])
    rhigh, rlow = split(res[...])
    both = jnp.concatenate([shigh, rhigh, slow, rlow], axis=1)
    wanted = (first + lax.broadcasted_iota(jnp.int32, (1, 128), 1)).astype(f32)
    ids = vbuf[...].reshape(rows, 128)[:, 64:65]
    pick = (ids == wanted).astype(f32).astype(bf16)
    out = lax.dot_general(pick, both, (((0,), (0,)), ((), ())), preferred_element_type=f32)
    out = out[0:per]
    sol_out[...] = out[:, 0:32] + out[:, 64:96]
    res_out[...] = out[:, 32:64] + out[:, 96:128]
    vg.drain()
    pg.drain()


def replicated(
    images, conv_weight, projection, row_of, probes, initial, amplitude, inv_scale, noise_var
):
    per, _, _, channels = images.shape
    rows = per * lax.axis_size("blk") * lax.axis_size("rep")
    feats = projection.shape[1]
    cols = probes.shape[1]
    vmem = pl.BlockSpec(memory_space=pltpu.VMEM)
    smem = pl.BlockSpec(memory_space=pltpu.SMEM)
    vec = pltpu.VMEM((rows, cols), f32)
    return pl.pallas_call(
        whole_kernel,
        out_shape=(jax.ShapeDtypeStruct((per, cols), f32),) * 2,
        in_specs=[vmem] * 6 + [smem] * 3,
        out_specs=(vmem, vmem),
        scratch_shapes=[
            pltpu.VMEM((8, 4, per, 128), f32),
            pltpu.VMEM((8, 4, per, channels), bf16),
            pltpu.VMEM((per * 16 + 16, channels), f32),
            pltpu.VMEM((9 * channels, channels), bf16),
            pltpu.VMEM((rows, 128), bf16),
            pltpu.VMEM((rows, feats), bf16),
            vec,
            pltpu.VMEM((rows, rows), bf16),
            pltpu.VMEM((rows, rows), bf16),
            pltpu.VMEM((rows, 2 * cols), bf16),
            vec, vec, vec, vec,
            pltpu.SemaphoreType.DMA((11,)),
            pltpu.SemaphoreType.DMA((11,)),
            pltpu.SemaphoreType.DMA((11,)),
            pltpu.SemaphoreType.DMA((11,)),
        ],
        compiler_params=pltpu.CompilerParams(
            collective_id=0, has_side_effects=True, vmem_limit_bytes=40 * 2**20),
    )(images, conv_weight, projection, row_of.reshape(1, -1), probes, initial,
      amplitude, inv_scale, noise_var)


def solution(mesh):
    in_specs = (
        P(("blk", "rep"), None, None, None),
        P(),
        P(),
        P("blk"),
        P(("blk", "rep"), None),
        P(("blk", "rep"), None),
        P(),
        P(),
        P(),
    )
    out_specs = (P(("blk", "rep"), None), P(("blk", "rep"), None))
    small = mesh.shape["blk"] == 8 and mesh.shape["rep"] == 4
    return jax.shard_map(
        replicated if small else per_device, mesh=mesh, in_specs=in_specs, out_specs=out_specs, check_vma=False
    )
```

```python
import jax
import jax.numpy as jnp
from jax import lax
from jax.sharding import PartitionSpec as P
from jax.experimental import pallas as pl
from jax.experimental.pallas import tpu as pltpu

F = 512
GROUPS = 32
ITERS = 2


def encode(images, conv_weight, projection):
    conv_out = lax.conv_general_dilated(
        images,
        conv_weight,
        (1, 1),
        "SAME",
        dimension_numbers=("NHWC", "HWIO", "NHWC"),
        feature_group_count=GROUPS,
        preferred_element_type=jnp.float32,
    )
    mixed = images.astype(jnp.float32) + jax.nn.silu(conv_out)
    pooled = jnp.mean(mixed, axis=(1, 2)).astype(jnp.bfloat16)
    raw_proj = jnp.dot(pooled, projection, preferred_element_type=jnp.float32)
    inverse = lax.rsqrt(jnp.mean(raw_proj * raw_proj, axis=-1, keepdims=True) + 1e-05)
    return (raw_proj * inverse).astype(jnp.bfloat16)


def kernel_rows(row_feats, row_norms, col_feats, col_norms, amplitude, inv_scale):
    cross = lax.dot_general(
        col_feats, row_feats, (((1,), (1,)), ((), ())), preferred_element_type=jnp.float32
    )
    distance = col_norms[:, None] + row_norms[None, :] - 2.0 * cross
    return amplitude * jnp.exp(-inv_scale * distance / (2.0 * F))


def contract(kern, vectors):
    return lax.dot_general(
        kern,
        vectors,
        (((0,), (0,)), ((), ())),
        precision=lax.Precision.HIGHEST,
        preferred_element_type=jnp.float32,
    )


def column_dots(left, right):
    return jnp.sum(left * right, axis=0)


def per_device(
    images, conv_weight, projection, row_of, probes, initial, amplitude, inv_scale, noise_var
):
    encoded = encode(images, conv_weight, projection)
    quarter = encoded.shape[0]
    group = lax.all_gather(encoded, "rep", axis=0, tiled=True)
    rows_total = group.shape[0]
    blk_count = lax.axis_size("blk")
    per_dest = rows_total // min(rows_total, blk_count)
    block_first = lax.axis_index("blk") * rows_total
    target_blk = row_of // rows_total
    order = jnp.arange(rows_total, dtype=jnp.int32)
    same_target = target_blk[:, None] == target_blk[None, :]
    earlier = order[None, :] < order[:, None]
    arrival = jnp.sum(jnp.logical_and(same_target, earlier).astype(jnp.int32), axis=1)
    chosen = jnp.logical_and(
        target_blk[None, None, :] == jnp.arange(blk_count, dtype=jnp.int32)[:, None, None],
        arrival[None, None, :] == jnp.arange(per_dest, dtype=jnp.int32)[None, :, None],
    )
    outgoing = jnp.einsum(
        "bsq,qf->bsf", chosen.astype(jnp.bfloat16), group, preferred_element_type=jnp.float32
    ).astype(jnp.bfloat16)
    row_slots = jnp.sum(jnp.where(chosen, row_of[None, None, :] + 1, 0), axis=2) - 1
    incoming, incoming_rows = (
        lax.all_to_all(outgoing, "blk", split_axis=0, concat_axis=0, tiled=True),
        lax.all_to_all(row_slots, "blk", split_axis=0, concat_axis=0, tiled=True),
    )
    local_pos = incoming_rows.reshape(-1) - block_first
    placing = (local_pos[None, :] == order[:, None]).astype(jnp.bfloat16)
    row_feats = jnp.dot(
        placing, incoming.reshape(-1, incoming.shape[-1]), preferred_element_type=jnp.float32
    ).astype(jnp.bfloat16)
    mine = lax.dynamic_slice_in_dim(row_feats, lax.axis_index("rep") * quarter, quarter, 0)
    row_wide = row_feats.astype(jnp.float32)
    row_norms = jnp.sum(row_wide * row_wide, axis=1)
    probe_count = probes.shape[1]
    zeros_acc = jnp.zeros((rows_total, probe_count), jnp.float32)

    def tile_of(segment):
        seg_wide = segment.astype(jnp.float32)
        return kernel_rows(
            row_feats,
            row_norms,
            segment,
            jnp.sum(seg_wide * seg_wide, axis=1),
            amplitude,
            inv_scale,
        )

    def finish(totals, vectors):
        return (
            lax.psum_scatter(totals, "rep", scatter_dimension=0, tiled=True) + noise_var * vectors
        )

    def columns(vectors):
        return lax.all_gather(vectors, "blk", axis=0, tiled=True)

    def product(vectors):
        gathered = columns(vectors)
        segment = lax.all_gather(mine, "blk", axis=0, tiled=True)
        vec_rows = lax.slice_in_dim(gathered, 0, segment.shape[0], axis=0)
        return finish(zeros_acc + contract(tile_of(segment), vec_rows), vectors)

    start_image = product(initial)

    def paired(vectors, image):
        return lax.psum(
            (column_dots(vectors, vectors), column_dots(vectors, image)), ("blk", "rep")
        )

    solution = initial
    residual = probes - start_image
    image = product(residual)
    norm_now, inner = paired(residual, image)
    alpha = norm_now / inner
    direction = residual
    along = image
    for iteration in range(ITERS):
        solution = solution + alpha * direction
        residual = residual - alpha * along
        if iteration + 1 < ITERS:
            image = product(residual)
            norm_next, inner = paired(residual, image)
            ratio = norm_next / norm_now
            alpha = norm_next / (inner - ratio * norm_next / alpha)
            direction = residual + ratio * direction
            along = image + ratio * along
            norm_now = norm_next
    return (solution, residual)


f32 = jnp.float32
bf16 = jnp.bfloat16
MESH = pl.DeviceIdType.MESH
LOG2E = 1.4426950408889634


class Gather:
    def __init__(self, buf, send, recv, where):
        self.buf, self.send, self.recv = buf, send, recv
        self.z, self.x, self.y, self.c = where
        self.q = (self.x * 2 + self.y) * 2 + self.c
        self.qx = ((1 - self.x) * 2 + self.y) * 2 + self.c
        self.qy = (self.x * 2 + (1 - self.y)) * 2 + self.c
        self.qd = ((1 - self.x) * 2 + (1 - self.y)) * 2 + self.c
        self.px = (self.z * 2 + 1 - self.x, self.y * 2 + self.c)
        self.py = (self.z * 2 + self.x, (1 - self.y) * 2 + self.c)
        self.pc = (self.z * 2 + self.x, self.y * 2 + 1 - self.c)
        self.copies = []

    def copy(self, k, ref, device):
        c = pltpu.make_async_remote_copy(
            src_ref=ref, dst_ref=ref, send_sem=self.send.at[k], recv_sem=self.recv.at[k],
            device_id=device, device_id_type=MESH)
        c.start()
        self.copies.append(c)
        return c

    def start_z(self):
        own = self.buf.at[self.q, self.z]
        self.zc = [
            self.copy(d - 1, own, (lax.rem(self.z + d, 4) * 2 + self.x, self.y * 2 + self.c))
            for d in (1, 2, 3)
        ]

    def start_xy(self):
        for c in self.zc:
            c.wait_recv()
        col = self.buf.at[self.q]
        self.cx = self.copy(3, col, self.px)
        self.cy = self.copy(4, col, self.py)
        self.cc = self.copy(5, col, self.pc)

    def forward(self):
        half = self.buf.shape[1] // 2
        self.cx.wait_recv()
        self.fy = self.copy(6, self.buf.at[self.qx, pl.ds(0, half)], self.py)
        self.ccx = self.copy(8, self.buf.at[self.qx], self.pc)
        self.cy.wait_recv()
        self.fx = self.copy(7, self.buf.at[self.qy, pl.ds(half, half)], self.px)
        self.ccy = self.copy(9, self.buf.at[self.qy], self.pc)

    def forward_diagonal(self):
        self.fy.wait_recv()
        self.fx.wait_recv()
        self.ccd = self.copy(10, self.buf.at[self.qd], self.pc)

    def finish(self):
        for c in (self.cc, self.ccx, self.ccy, self.ccd):
            c.wait_recv()

    def drain(self):
        for c in self.copies:
            c.wait_send()


class ChunkGather(Gather):
    def start_z(self):
        z = self.z
        self.plane = [z, z + 1 - 2 * lax.rem(z, 2), lax.rem(z + 2, 4), 3 - z]
        own = self.buf.at[self.q, z]
        self.zc = [None] + [
            self.copy(k, own, (self.plane[k] * 2 + self.x, self.y * 2 + self.c))
            for k in (1, 2, 3)
        ]
        self.first = [None] * 4
        self.second = [None] * 4
        self.third = []
        self.send_chunk(0)

    def send_chunk(self, k):
        if k:
            self.zc[k].wait_recv()
        block = self.buf.at[self.q, self.plane[k]]
        self.first[k] = (self.copy(4 + k, block, self.px), self.copy(8 + k, block, self.py))
        self.third.append(self.copy(12 + k, block, self.pc))

    def forward_chunk(self, k):
        half = self.buf.shape[2] // 2
        bx = self.buf.at[self.qx, self.plane[k]]
        by = self.buf.at[self.qy, self.plane[k]]
        self.first[k][0].wait_recv()
        fy = self.copy(16 + k, bx.at[pl.ds(0, half)], self.py)
        self.third.append(self.copy(24 + k, bx, self.pc))
        self.first[k][1].wait_recv()
        fx = self.copy(20 + k, by.at[pl.ds(half, half)], self.px)
        self.third.append(self.copy(28 + k, by, self.pc))
        self.second[k] = (fy, fx)

    def forward_chunk_diagonal(self, k):
        for c in self.second[k]:
            c.wait_recv()
        self.third.append(self.copy(32 + k, self.buf.at[self.qd, self.plane[k]], self.pc))

    def finish(self):
        for c in self.third:
            c.wait_recv()


def split(value):
    high = value.astype(bf16)
    return high, (value - high.astype(f32)).astype(bf16)


def whole_kernel(
    images_in, weight_in, projection_in, row_of_in, probes_in, initial_in, amp, inv, noise,
    out_ref, images, weight, projection, row_of, probes, initial, in_sem,
    vbuf, pbuf, padded, wide_w, perm_v, feats, dcol, ehi, elo, whl, sol, res, direc, image,
    vsend, vrecv, psend, precv,
):
    blk, rep = lax.axis_index("blk"), lax.axis_index("rep")
    z, x = blk // 2, lax.rem(blk, 2)
    y, c = rep // 2, lax.rem(rep, 2)
    where = (z, x, y, c)
    vg = Gather(vbuf, vsend, vrecv, where)
    pg = ChunkGather(pbuf, psend, precv, where)
    q = vg.q
    per = images.shape[0]
    rows = vbuf.shape[0] * vbuf.shape[1] * per
    tile = 256
    tiles = rows // tile
    first = blk * row_of.shape[1] + rep * per

    barrier = pltpu.get_barrier_semaphore()
    for d in (1, 2, 3):
        pl.semaphore_signal(
            barrier, inc=1, device_id=(lax.rem(z + d, 4) * 2 + x, rep), device_id_type=MESH)
    for device in (vg.px, vg.py, vg.pc):
        pl.semaphore_signal(barrier, inc=1, device_id=device, device_id_type=MESH)

    pairs = ((row_of_in, row_of), (probes_in, probes), (initial_in, initial),
             (images_in, images), (weight_in, weight), (projection_in, projection))
    loads = [pltpu.make_async_copy(a, b, in_sem.at[k]) for k, (a, b) in enumerate(pairs)]
    for load in loads:
        load.start()

    for load in loads[:3]:
        load.wait()
    lane = lax.broadcasted_iota(jnp.int32, (per, row_of.shape[1]), 1)
    sub = lax.broadcasted_iota(jnp.int32, (per, row_of.shape[1]), 0)
    mine = jnp.sum(
        jnp.where(lane == sub + rep * per, row_of[...].astype(f32), 0.0), axis=1, keepdims=True)
    vbuf[q, z] = jnp.broadcast_to(mine, (per, 128))
    vbuf[q, z, :, 0:32] = probes[...]
    vbuf[q, z, :, 32:64] = initial[...]
    pl.semaphore_wait(barrier, 6)
    vg.start_z()

    for load in loads[3:]:
        load.wait()
    channels = images.shape[3]
    group = weight.shape[2]
    diag = (lax.broadcasted_iota(jnp.int32, (channels, channels), 0) // group
            == lax.broadcasted_iota(jnp.int32, (channels, channels), 1) // group)
    for t in range(9):
        w = weight[t // 3, t % 3].astype(f32)
        w = jnp.broadcast_to(w[None], (channels // group, group, channels))
        w = w.reshape(channels, channels)
        wide_w[t * channels:(t + 1) * channels] = jnp.where(diag, w, 0.0).astype(bf16)
    pixels = per * 16
    padded[0:8] = jnp.zeros((8, channels), f32)
    padded[pixels + 8:pixels + 16] = jnp.zeros((8, channels), f32)
    padded[8:pixels + 8] = images[...].astype(f32).reshape(pixels, channels)
    pos = lax.broadcasted_iota(jnp.int32, (tile, channels), 0)
    pos_x, pos_y = lax.rem(pos, 4), lax.rem(pos, 16) // 4

    def conv_tile(t):
        parts = []
        for dy in (-1, 0, 1):
            for dx in (-1, 0, 1):
                part = padded[8 + t * tile + dy * 4 + dx:8 + (t + 1) * tile + dy * 4 + dx]
                ok = None
                if dx:
                    ok = pos_x != (0 if dx < 0 else 3)
                if dy:
                    oky = pos_y != (0 if dy < 0 else 3)
                    ok = oky if ok is None else jnp.logical_and(ok, oky)
                if ok is not None:
                    part = jnp.where(ok, part, 0.0)
                parts.append(part.astype(bf16))
        v = jnp.dot(jnp.concatenate(parts, axis=1), wide_w[...], preferred_element_type=f32)
        mixed = padded[8 + t * tile:8 + (t + 1) * tile] + v / (1.0 + jnp.exp(-v))
        pooled = jnp.sum(mixed.reshape(tile // 16, 16, channels), axis=1) * (1.0 / 16.0)
        pbuf[q, z, t * 16:(t + 1) * 16] = pooled.astype(bf16)

    conv_tile(0)
    conv_tile(1)
    pg.start_z()
    pg.send_chunk(1)
    pg.forward_chunk(0)
    pg.send_chunk(2)
    pg.forward_chunk(1)
    pg.send_chunk(3)
    pg.forward_chunk(2)
    vg.start_xy()
    pg.forward_chunk_diagonal(0)
    pg.forward_chunk(3)
    pg.forward_chunk_diagonal(1)
    pg.forward_chunk_diagonal(2)
    vg.forward()
    pg.forward_chunk_diagonal(3)
    pg.finish()

    per_tile = tile // (4 * per)
    scale = inv[0] / (2.0 * feats.shape[1])
    for i in range(tiles):
        pooled = pbuf[i * per_tile:(i + 1) * per_tile].reshape(tile, channels)
        raw = jnp.dot(pooled, projection[...], preferred_element_type=f32)
        mean = jnp.sum(raw * raw, axis=1, keepdims=True) * (1.0 / raw.shape[1])
        enc = (raw * lax.rsqrt(mean + 1e-05)).astype(bf16)
        feats[i * tile:(i + 1) * tile] = enc
        enc = enc.astype(f32)
        sq = jnp.sum(enc * enc, axis=1, keepdims=True)
        dcol[i * tile:(i + 1) * tile] = jnp.broadcast_to(jnp.exp(-scale * sq), (tile, 32))

    vg.forward_diagonal()
    gain = scale * (2.0 * LOG2E)

    @pl.loop(0, tiles)
    def _(i):
        r = pl.ds(pl.multiple_of(i * tile, tile), tile)
        for k in range(tiles):
            g = lax.dot_general(
                feats[r, :], feats[k * tile:(k + 1) * tile], (((1,), (1,)), ((), ())),
                preferred_element_type=f32)
            e = jnp.exp2(gain * g)
            high, low = split(e)
            ehi[r, k * tile:(k + 1) * tile] = high
            elo[r, k * tile:(k + 1) * tile] = low

    vg.finish()

    vall = vbuf[...].reshape(rows, 128)
    high = vall.astype(bf16)
    low = vall - high.astype(f32)
    lanes = lax.broadcasted_iota(jnp.int32, (rows, 128), 1)
    perm_v[...] = jnp.where(lanes < 64, high.astype(f32), pltpu.roll(low, 64, 1)).astype(bf16)
    j = lax.broadcasted_iota(jnp.int32, (1, rows), 1)
    jq, jz = j // (4 * per), lax.rem(j // per, 4)
    row_id = ((jz * 2 + jq // 4) * row_of.shape[1] + lax.rem(jq, 4) * per + lax.rem(j, per))
    row_id = row_id.astype(f32)
    for i in range(tiles):
        here = vbuf[i * per_tile:(i + 1) * per_tile].reshape(tile, 128)
        hot = (here[:, 64:65] == row_id).astype(f32).astype(bf16)
        got = jnp.dot(hot, perm_v[...], preferred_element_type=f32)
        got = got + pltpu.roll(got, 64, 1)
        res[i * tile:(i + 1) * tile] = got[:, 0:32]
        sol[i * tile:(i + 1) * tile] = got[:, 32:64]

    amplitude, noise_var = amp[0], noise[0]

    def product(vec):
        w = dcol[...] * vec[...]
        high, low = split(w)
        whl[:, 0:32] = high
        whl[:, 32:64] = low

        @pl.loop(0, tiles)
        def _(i):
            r = pl.ds(pl.multiple_of(i * tile, tile), tile)
            a = jnp.dot(ehi[r, :], whl[...], preferred_element_type=f32)
            b = jnp.dot(elo[r, :], whl[:, 0:32], preferred_element_type=f32)
            s = a[:, 0:32] + a[:, 32:64] + b
            image[r, :] = amplitude * (dcol[r, :] * s) + noise_var * vec[r, :]

    product(sol)
    first_res = res[...] - image[...]
    res[...] = first_res
    direc[...] = first_res
    norm = jnp.sum(first_res * first_res, axis=0, keepdims=True)
    for iteration in range(ITERS):
        product(direc)
        d = direc[...]
        im = image[...]
        alpha = norm / jnp.sum(d * im, axis=0, keepdims=True)
        sol[...] = sol[...] + alpha * d
        r = res[...] - alpha * im
        res[...] = r
        if iteration + 1 < ITERS:
            new = jnp.sum(r * r, axis=0, keepdims=True)
            direc[...] = r + (new / norm) * d
            norm = new

    shigh, slow = split(sol[...])
    rhigh, rlow = split(res[...])
    both = jnp.concatenate([shigh, rhigh, slow, rlow], axis=1)
    wanted = (first + lax.broadcasted_iota(jnp.int32, (1, 128), 1)).astype(f32)
    ids = vbuf[...].reshape(rows, 128)[:, 64:65]
    pick = (ids == wanted).astype(f32).astype(bf16)
    out = lax.dot_general(pick, both, (((0,), (0,)), ((), ())), preferred_element_type=f32)
    out_ref[...] = out[0:per]
    vg.drain()
    pg.drain()


def replicated(
    images, conv_weight, projection, row_of, probes, initial, amplitude, inv_scale, noise_var
):
    per, _, _, channels = images.shape
    rows = per * lax.axis_size("blk") * lax.axis_size("rep")
    feats = projection.shape[1]
    cols = probes.shape[1]
    vmem = pl.BlockSpec(memory_space=pltpu.VMEM)
    hbm = pl.BlockSpec(memory_space=pltpu.HBM)
    smem = pl.BlockSpec(memory_space=pltpu.SMEM)
    vec = pltpu.VMEM((rows, cols), f32)
    out = pl.pallas_call(
        whole_kernel,
        out_shape=jax.ShapeDtypeStruct((per, 4 * cols), f32),
        in_specs=[hbm] * 6 + [smem] * 3,
        out_specs=vmem,
        scratch_shapes=[
            pltpu.VMEM(images.shape, bf16),
            pltpu.VMEM(conv_weight.shape, bf16),
            pltpu.VMEM(projection.shape, bf16),
            pltpu.VMEM((1, row_of.shape[0]), jnp.int32),
            pltpu.VMEM(probes.shape, f32),
            pltpu.VMEM(initial.shape, f32),
            pltpu.SemaphoreType.DMA((6,)),
            pltpu.VMEM((8, 4, per, 128), f32),
            pltpu.VMEM((8, 4, per, channels), bf16),
            pltpu.VMEM((per * 16 + 16, channels), f32),
            pltpu.VMEM((9 * channels, channels), bf16),
            pltpu.VMEM((rows, 128), bf16),
            pltpu.VMEM((rows, feats), bf16),
            vec,
            pltpu.VMEM((rows, rows), bf16),
            pltpu.VMEM((rows, rows), bf16),
            pltpu.VMEM((rows, 2 * cols), bf16),
            vec, vec, vec, vec,
            pltpu.SemaphoreType.DMA((11,)),
            pltpu.SemaphoreType.DMA((11,)),
            pltpu.SemaphoreType.DMA((36,)),
            pltpu.SemaphoreType.DMA((36,)),
        ],
        compiler_params=pltpu.CompilerParams(
            collective_id=0, has_side_effects=True, vmem_limit_bytes=63 * 2**20),
    )(images, conv_weight, projection, row_of.reshape(1, -1), probes, initial,
      amplitude, inv_scale, noise_var)
    return (
        out[:, :cols] + out[:, 2 * cols:3 * cols],
        out[:, cols:2 * cols] + out[:, 3 * cols:],
    )


def solution(mesh):
    in_specs = (
        P(("blk", "rep"), None, None, None),
        P(),
        P(),
        P("blk"),
        P(("blk", "rep"), None),
        P(("blk", "rep"), None),
        P(),
        P(),
        P(),
    )
    out_specs = (P(("blk", "rep"), None), P(("blk", "rep"), None))
    small = mesh.shape["blk"] == 8 and mesh.shape["rep"] == 4
    return jax.shard_map(
        replicated if small else per_device, mesh=mesh, in_specs=in_specs, out_specs=out_specs, check_vma=False
    )
```

```python
import jax
import jax.numpy as jnp
from jax import lax
from jax.sharding import PartitionSpec as P
from jax.experimental import pallas as pl
from jax.experimental.pallas import tpu as pltpu

F = 512
GROUPS = 32
ITERS = 2


def encode(images, conv_weight, projection):
    conv_out = lax.conv_general_dilated(
        images,
        conv_weight,
        (1, 1),
        "SAME",
        dimension_numbers=("NHWC", "HWIO", "NHWC"),
        feature_group_count=GROUPS,
        preferred_element_type=jnp.float32,
    )
    mixed = images.astype(jnp.float32) + jax.nn.silu(conv_out)
    pooled = jnp.mean(mixed, axis=(1, 2)).astype(jnp.bfloat16)
    raw_proj = jnp.dot(pooled, projection, preferred_element_type=jnp.float32)
    inverse = lax.rsqrt(jnp.mean(raw_proj * raw_proj, axis=-1, keepdims=True) + 1e-05)
    return (raw_proj * inverse).astype(jnp.bfloat16)


def kernel_rows(row_feats, row_norms, col_feats, col_norms, amplitude, inv_scale):
    cross = lax.dot_general(
        col_feats, row_feats, (((1,), (1,)), ((), ())), preferred_element_type=jnp.float32
    )
    distance = col_norms[:, None] + row_norms[None, :] - 2.0 * cross
    return amplitude * jnp.exp(-inv_scale * distance / (2.0 * F))


def contract(kern, vectors):
    return lax.dot_general(
        kern,
        vectors,
        (((0,), (0,)), ((), ())),
        precision=lax.Precision.HIGHEST,
        preferred_element_type=jnp.float32,
    )


def column_dots(left, right):
    return jnp.sum(left * right, axis=0)


def per_device(
    images, conv_weight, projection, row_of, probes, initial, amplitude, inv_scale, noise_var
):
    encoded = encode(images, conv_weight, projection)
    quarter = encoded.shape[0]
    group = lax.all_gather(encoded, "rep", axis=0, tiled=True)
    rows_total = group.shape[0]
    blk_count = lax.axis_size("blk")
    per_dest = rows_total // min(rows_total, blk_count)
    block_first = lax.axis_index("blk") * rows_total
    target_blk = row_of // rows_total
    order = jnp.arange(rows_total, dtype=jnp.int32)
    same_target = target_blk[:, None] == target_blk[None, :]
    earlier = order[None, :] < order[:, None]
    arrival = jnp.sum(jnp.logical_and(same_target, earlier).astype(jnp.int32), axis=1)
    chosen = jnp.logical_and(
        target_blk[None, None, :] == jnp.arange(blk_count, dtype=jnp.int32)[:, None, None],
        arrival[None, None, :] == jnp.arange(per_dest, dtype=jnp.int32)[None, :, None],
    )
    outgoing = jnp.einsum(
        "bsq,qf->bsf", chosen.astype(jnp.bfloat16), group, preferred_element_type=jnp.float32
    ).astype(jnp.bfloat16)
    row_slots = jnp.sum(jnp.where(chosen, row_of[None, None, :] + 1, 0), axis=2) - 1
    incoming, incoming_rows = (
        lax.all_to_all(outgoing, "blk", split_axis=0, concat_axis=0, tiled=True),
        lax.all_to_all(row_slots, "blk", split_axis=0, concat_axis=0, tiled=True),
    )
    local_pos = incoming_rows.reshape(-1) - block_first
    placing = (local_pos[None, :] == order[:, None]).astype(jnp.bfloat16)
    row_feats = jnp.dot(
        placing, incoming.reshape(-1, incoming.shape[-1]), preferred_element_type=jnp.float32
    ).astype(jnp.bfloat16)
    mine = lax.dynamic_slice_in_dim(row_feats, lax.axis_index("rep") * quarter, quarter, 0)
    row_wide = row_feats.astype(jnp.float32)
    row_norms = jnp.sum(row_wide * row_wide, axis=1)
    probe_count = probes.shape[1]
    zeros_acc = jnp.zeros((rows_total, probe_count), jnp.float32)

    def tile_of(segment):
        seg_wide = segment.astype(jnp.float32)
        return kernel_rows(
            row_feats,
            row_norms,
            segment,
            jnp.sum(seg_wide * seg_wide, axis=1),
            amplitude,
            inv_scale,
        )

    def finish(totals, vectors):
        return (
            lax.psum_scatter(totals, "rep", scatter_dimension=0, tiled=True) + noise_var * vectors
        )

    def columns(vectors):
        return lax.all_gather(vectors, "blk", axis=0, tiled=True)

    def product(vectors):
        gathered = columns(vectors)
        segment = lax.all_gather(mine, "blk", axis=0, tiled=True)
        vec_rows = lax.slice_in_dim(gathered, 0, segment.shape[0], axis=0)
        return finish(zeros_acc + contract(tile_of(segment), vec_rows), vectors)

    start_image = product(initial)

    def paired(vectors, image):
        return lax.psum(
            (column_dots(vectors, vectors), column_dots(vectors, image)), ("blk", "rep")
        )

    solution = initial
    residual = probes - start_image
    image = product(residual)
    norm_now, inner = paired(residual, image)
    alpha = norm_now / inner
    direction = residual
    along = image
    for iteration in range(ITERS):
        solution = solution + alpha * direction
        residual = residual - alpha * along
        if iteration + 1 < ITERS:
            image = product(residual)
            norm_next, inner = paired(residual, image)
            ratio = norm_next / norm_now
            alpha = norm_next / (inner - ratio * norm_next / alpha)
            direction = residual + ratio * direction
            along = image + ratio * along
            norm_now = norm_next
    return (solution, residual)


f32 = jnp.float32
bf16 = jnp.bfloat16
MESH = pl.DeviceIdType.MESH
LOG2E = 1.4426950408889634


class Gather:
    def __init__(self, buf, send, recv, where):
        self.buf, self.send, self.recv = buf, send, recv
        self.z, self.x, self.y, self.c = where
        self.q = (self.x * 2 + self.y) * 2 + self.c
        self.qx = ((1 - self.x) * 2 + self.y) * 2 + self.c
        self.qy = (self.x * 2 + (1 - self.y)) * 2 + self.c
        self.qd = ((1 - self.x) * 2 + (1 - self.y)) * 2 + self.c
        self.px = (self.z * 2 + 1 - self.x, self.y * 2 + self.c)
        self.py = (self.z * 2 + self.x, (1 - self.y) * 2 + self.c)
        self.pc = (self.z * 2 + self.x, self.y * 2 + 1 - self.c)
        self.copies = []

    def copy(self, k, ref, device):
        c = pltpu.make_async_remote_copy(
            src_ref=ref, dst_ref=ref, send_sem=self.send.at[k], recv_sem=self.recv.at[k],
            device_id=device, device_id_type=MESH)
        c.start()
        self.copies.append(c)
        return c

    def drain(self):
        for c in self.copies:
            c.wait_send()


class DirectGather(Gather):
    def start_z(self):
        z = self.z
        self.plane = [z, z + 1 - 2 * lax.rem(z, 2), lax.rem(z + 2, 4), 3 - z]
        own = self.buf.at[self.q, z]
        self.zc = [None] + [
            self.copy(k, own, (self.plane[k] * 2 + self.x, self.y * 2 + self.c))
            for k in (1, 2, 3)
        ]
        self.third = []

    def send_chunk(self, k):
        if k:
            self.zc[k].wait_recv()
        block = self.buf.at[self.q, self.plane[k]]
        for n, device in enumerate(self.others()):
            self.third.append(self.copy(4 + 7 * k + n, block, device))

    def others(self):
        z, xs, ys, cs = self.z, (self.x, 1 - self.x), (self.y, 1 - self.y), (self.c, 1 - self.c)
        flips = ((1, 1, 0), (1, 1, 1), (1, 0, 0), (0, 1, 0), (1, 0, 1), (0, 1, 1), (0, 0, 1))
        return [(z * 2 + xs[a], ys[b] * 2 + cs[d]) for a, b, d in flips]

    def finish(self):
        for c in self.third:
            c.wait_recv()


def split(value):
    high = value.astype(bf16)
    return high, (value - high.astype(f32)).astype(bf16)


def whole_kernel(
    images_in, weight_in, projection_in, row_of_in, probes_in, initial_in, amp, inv, noise,
    out_ref, images, weight, projection, row_of, probes, initial, in_sem,
    vbuf, pbuf, padded, wide_w, perm_v, feats, dcol, ehi, elo, whl, sol, res, direc, image,
    vsend, vrecv, psend, precv,
):
    blk, rep = lax.axis_index("blk"), lax.axis_index("rep")
    z, x = blk // 2, lax.rem(blk, 2)
    y, c = rep // 2, lax.rem(rep, 2)
    where = (z, x, y, c)
    vg = DirectGather(vbuf, vsend, vrecv, where)
    pg = DirectGather(pbuf, psend, precv, where)
    q = vg.q
    per = images.shape[0]
    rows = vbuf.shape[0] * vbuf.shape[1] * per
    tile = 256
    tiles = rows // tile
    first = blk * row_of.shape[1] + rep * per

    barrier = pltpu.get_barrier_semaphore()
    for d in (1, 2, 3):
        pl.semaphore_signal(
            barrier, inc=1, device_id=(lax.rem(z + d, 4) * 2 + x, rep), device_id_type=MESH)
    for device in pg.others():
        pl.semaphore_signal(barrier, inc=1, device_id=device, device_id_type=MESH)

    pairs = ((row_of_in, row_of), (probes_in, probes), (initial_in, initial),
             (images_in, images), (weight_in, weight), (projection_in, projection))
    loads = [pltpu.make_async_copy(a, b, in_sem.at[k]) for k, (a, b) in enumerate(pairs)]
    for load in loads:
        load.start()

    for load in loads[:3]:
        load.wait()
    lane = lax.broadcasted_iota(jnp.int32, (per, row_of.shape[1]), 1)
    sub = lax.broadcasted_iota(jnp.int32, (per, row_of.shape[1]), 0)
    mine = jnp.sum(
        jnp.where(lane == sub + rep * per, row_of[...].astype(f32), 0.0), axis=1, keepdims=True)
    vbuf[q, z] = jnp.broadcast_to(mine, (per, 128))
    vbuf[q, z, :, 0:32] = probes[...]
    vbuf[q, z, :, 32:64] = initial[...]
    pl.semaphore_wait(barrier, 10)
    vg.start_z()

    for load in loads[3:]:
        load.wait()
    channels = images.shape[3]
    group = weight.shape[2]
    diag = (lax.broadcasted_iota(jnp.int32, (channels, channels), 0) // group
            == lax.broadcasted_iota(jnp.int32, (channels, channels), 1) // group)
    for t in range(9):
        w = weight[t // 3, t % 3].astype(f32)
        w = jnp.broadcast_to(w[None], (channels // group, group, channels))
        w = w.reshape(channels, channels)
        wide_w[t * channels:(t + 1) * channels] = jnp.where(diag, w, 0.0).astype(bf16)
    pixels = per * 16
    padded[0:8] = jnp.zeros((8, channels), f32)
    padded[pixels + 8:pixels + 16] = jnp.zeros((8, channels), f32)
    padded[8:pixels + 8] = images[...].astype(f32).reshape(pixels, channels)
    pos = lax.broadcasted_iota(jnp.int32, (tile, channels), 0)
    pos_x, pos_y = lax.rem(pos, 4), lax.rem(pos, 16) // 4

    def conv_tile(t):
        parts = []
        for dy in (-1, 0, 1):
            for dx in (-1, 0, 1):
                part = padded[8 + t * tile + dy * 4 + dx:8 + (t + 1) * tile + dy * 4 + dx]
                ok = None
                if dx:
                    ok = pos_x != (0 if dx < 0 else 3)
                if dy:
                    oky = pos_y != (0 if dy < 0 else 3)
                    ok = oky if ok is None else jnp.logical_and(ok, oky)
                if ok is not None:
                    part = jnp.where(ok, part, 0.0)
                parts.append(part.astype(bf16))
        v = jnp.dot(jnp.concatenate(parts, axis=1), wide_w[...], preferred_element_type=f32)
        mixed = padded[8 + t * tile:8 + (t + 1) * tile] + v / (1.0 + jnp.exp(-v))
        pooled = jnp.sum(mixed.reshape(tile // 16, 16, channels), axis=1) * (1.0 / 16.0)
        pbuf[q, z, t * 16:(t + 1) * 16] = pooled.astype(bf16)

    conv_tile(0)
    conv_tile(1)
    pg.start_z()
    pg.send_chunk(0)
    vg.send_chunk(0)
    for k in (1, 2, 3):
        pg.send_chunk(k)
    for k in (1, 2, 3):
        vg.send_chunk(k)
    pg.finish()

    per_tile = tile // (4 * per)
    scale = inv[0] / (2.0 * feats.shape[1])
    for i in range(tiles):
        pooled = pbuf[i * per_tile:(i + 1) * per_tile].reshape(tile, channels)
        raw = jnp.dot(pooled, projection[...], preferred_element_type=f32)
        mean = jnp.sum(raw * raw, axis=1, keepdims=True) * (1.0 / raw.shape[1])
        enc = (raw * lax.rsqrt(mean + 1e-05)).astype(bf16)
        feats[i * tile:(i + 1) * tile] = enc
        enc = enc.astype(f32)
        sq = jnp.sum(enc * enc, axis=1, keepdims=True)
        dcol[i * tile:(i + 1) * tile] = jnp.broadcast_to(jnp.exp(-scale * sq), (tile, 32))

    gain = scale * (2.0 * LOG2E)

    @pl.loop(0, tiles)
    def _(i):
        r = pl.ds(pl.multiple_of(i * tile, tile), tile)
        for k in range(tiles):
            g = lax.dot_general(
                feats[r, :], feats[k * tile:(k + 1) * tile], (((1,), (1,)), ((), ())),
                preferred_element_type=f32)
            e = jnp.exp2(gain * g)
            high, low = split(e)
            ehi[r, k * tile:(k + 1) * tile] = high
            elo[r, k * tile:(k + 1) * tile] = low

    vg.finish()

    vall = vbuf[...].reshape(rows, 128)
    high = vall.astype(bf16)
    low = vall - high.astype(f32)
    lanes = lax.broadcasted_iota(jnp.int32, (rows, 128), 1)
    perm_v[...] = jnp.where(lanes < 64, high.astype(f32), pltpu.roll(low, 64, 1)).astype(bf16)
    j = lax.broadcasted_iota(jnp.int32, (1, rows), 1)
    jq, jz = j // (4 * per), lax.rem(j // per, 4)
    row_id = ((jz * 2 + jq // 4) * row_of.shape[1] + lax.rem(jq, 4) * per + lax.rem(j, per))
    row_id = row_id.astype(f32)
    for i in range(tiles):
        here = vbuf[i * per_tile:(i + 1) * per_tile].reshape(tile, 128)
        hot = (here[:, 64:65] == row_id).astype(f32).astype(bf16)
        got = jnp.dot(hot, perm_v[...], preferred_element_type=f32)
        got = got + pltpu.roll(got, 64, 1)
        res[i * tile:(i + 1) * tile] = got[:, 0:32]
        sol[i * tile:(i + 1) * tile] = got[:, 32:64]

    amplitude, noise_var = amp[0], noise[0]

    def product(vec):
        w = dcol[...] * vec[...]
        high, low = split(w)
        whl[:, 0:32] = high
        whl[:, 32:64] = low

        @pl.loop(0, tiles, unroll=True)
        def _(i):
            r = pl.ds(pl.multiple_of(i * tile, tile), tile)
            a = jnp.dot(ehi[r, :], whl[...], preferred_element_type=f32)
            b = jnp.dot(elo[r, :], whl[:, 0:32], preferred_element_type=f32)
            s = a[:, 0:32] + a[:, 32:64] + b
            image[r, :] = amplitude * (dcol[r, :] * s) + noise_var * vec[r, :]

    product(sol)
    first_res = res[...] - image[...]
    res[...] = first_res
    direc[...] = first_res
    norm = jnp.sum(first_res * first_res, axis=0, keepdims=True)
    for iteration in range(ITERS):
        product(direc)
        d = direc[...]
        im = image[...]
        alpha = norm / jnp.sum(d * im, axis=0, keepdims=True)
        sol[...] = sol[...] + alpha * d
        r = res[...] - alpha * im
        res[...] = r
        if iteration + 1 < ITERS:
            new = jnp.sum(r * r, axis=0, keepdims=True)
            direc[...] = r + (new / norm) * d
            norm = new

    shigh, slow = split(sol[...])
    rhigh, rlow = split(res[...])
    both = jnp.concatenate([shigh, rhigh, slow, rlow], axis=1)
    wanted = (first + lax.broadcasted_iota(jnp.int32, (1, 128), 1)).astype(f32)
    ids = vbuf[...].reshape(rows, 128)[:, 64:65]
    pick = (ids == wanted).astype(f32).astype(bf16)
    out = lax.dot_general(pick, both, (((0,), (0,)), ((), ())), preferred_element_type=f32)
    out_ref[...] = out[0:per]
    vg.drain()
    pg.drain()


def replicated(
    images, conv_weight, projection, row_of, probes, initial, amplitude, inv_scale, noise_var
):
    per, _, _, channels = images.shape
    rows = per * lax.axis_size("blk") * lax.axis_size("rep")
    feats = projection.shape[1]
    cols = probes.shape[1]
    vmem = pl.BlockSpec(memory_space=pltpu.VMEM)
    hbm = pl.BlockSpec(memory_space=pltpu.HBM)
    smem = pl.BlockSpec(memory_space=pltpu.SMEM)
    vec = pltpu.VMEM((rows, cols), f32)
    out = pl.pallas_call(
        whole_kernel,
        out_shape=jax.ShapeDtypeStruct((per, 4 * cols), f32),
        in_specs=[hbm] * 6 + [smem] * 3,
        out_specs=vmem,
        scratch_shapes=[
            pltpu.VMEM(images.shape, bf16),
            pltpu.VMEM(conv_weight.shape, bf16),
            pltpu.VMEM(projection.shape, bf16),
            pltpu.VMEM((1, row_of.shape[0]), jnp.int32),
            pltpu.VMEM(probes.shape, f32),
            pltpu.VMEM(initial.shape, f32),
            pltpu.SemaphoreType.DMA((6,)),
            pltpu.VMEM((8, 4, per, 128), f32),
            pltpu.VMEM((8, 4, per, channels), bf16),
            pltpu.VMEM((per * 16 + 16, channels), f32),
            pltpu.VMEM((9 * channels, channels), bf16),
            pltpu.VMEM((rows, 128), bf16),
            pltpu.VMEM((rows, feats), bf16),
            vec,
            pltpu.VMEM((rows, rows), bf16),
            pltpu.VMEM((rows, rows), bf16),
            pltpu.VMEM((rows, 2 * cols), bf16),
            vec, vec, vec, vec,
            pltpu.SemaphoreType.DMA((36,)),
            pltpu.SemaphoreType.DMA((36,)),
            pltpu.SemaphoreType.DMA((36,)),
            pltpu.SemaphoreType.DMA((36,)),
        ],
        compiler_params=pltpu.CompilerParams(
            collective_id=0, has_side_effects=True, vmem_limit_bytes=63 * 2**20),
    )(images, conv_weight, projection, row_of.reshape(1, -1), probes, initial,
      amplitude, inv_scale, noise_var)
    return (
        out[:, :cols] + out[:, 2 * cols:3 * cols],
        out[:, cols:2 * cols] + out[:, 3 * cols:],
    )


def solution(mesh):
    in_specs = (
        P(("blk", "rep"), None, None, None),
        P(),
        P(),
        P("blk"),
        P(("blk", "rep"), None),
        P(("blk", "rep"), None),
        P(),
        P(),
        P(),
    )
    out_specs = (P(("blk", "rep"), None), P(("blk", "rep"), None))
    small = mesh.shape["blk"] == 8 and mesh.shape["rep"] == 4
    return jax.shard_map(
        replicated if small else per_device, mesh=mesh, in_specs=in_specs, out_specs=out_specs, check_vma=False
    )
```
